512 devices in a mesh: dp: 4 (over x), expert: 32 (over y, z_hi, core), tensor: 4 (over z_lo).
Axes of the slice: x: 4, y: 4, z: 16 (z_hi: 4, z_lo: 4; z = z_hi * 4 + z_lo), core: 2. Of those that a mesh axis runs over, the one named last changes fastest.
Arguments:
- patches: bfloat16 [128, 576, 1280], P(('dp', 'expert'), None, 'tensor'), may hold values from -6 to 6
- router: bfloat16 [1280, 32], P('tensor'), may hold values from -0.15625 to 0.15625
- logits: float32 [128, 32, 576], P(('dp', 'expert')), may hold values from -16 to 260, as said below
- slot_outputs: bfloat16 [128, 32, 1280], P(('dp', 'expert'), None, 'tensor'), may hold values from -6 to 6
- cotangent: bfloat16 [128, 576, 1280], P(('dp', 'expert'), None, 'tensor'), may hold values from -6 to 6
- weight_in: bfloat16 [32, 1280, 5120], P('expert', None, ('dp', 'tensor')), may hold values from -0.15625 to 0.15625
- weight_out: bfloat16 [32, 5120, 1280], P('expert', ('dp', 'tensor')), may hold values from -0.078125 to 0.078125
Outputs:
- grad_patches: bfloat16 [128, 576, 1280], P(('dp', 'expert'), None, 'tensor')
- grad_router: float32 [1280, 32], P('tensor')
- grad_in: bfloat16 [32, 1280, 5120], P('expert', None, ('dp', 'tensor'))
- grad_out: bfloat16 [32, 5120, 1280], P('expert', ('dp', 'tensor'))
The draws below stay inside these ranges and needn't reach their ends.
Inputs may be any that keep to these rules, and one draw needn't show every extreme that they name: Saved router logits; each row of either softmax has a finite largest entry.
All inputs are finite; a program needn't handle non-finite values.
Results may differ from the reference program's by a relative error of at most 0.0085.
Values may be sent and summed in bfloat16 or wider, within the bound.
No kernel may reach another device: no remote copies, remote signals or barrier semaphores. Data moves between devices by JAX's collectives and lax.ppermute only.
A program may use at most 64 MiB of HBM per device.

```python
import jax
import jax.numpy as jnp
from jax import lax

D = 1280
FF = 5120
PATCHES = 576
EXPERTS = 32
IMAGES = 128


def draw_logits(key, part):
    key = jax.random.fold_in(key, 11)
    base_key = jax.random.fold_in(key, 0)
    return jnp.clip(2.0 * jax.random.normal(base_key, (IMAGES, EXPERTS, PATCHES), jnp.float32), -12.0, 12.0)


def block_scale(key, extent, pieces, least, high):
    gain = 1.0
    for position, parts in pieces:
        steps = jax.random.uniform(jax.random.fold_in(jax.random.fold_in(key, 6), position), (parts,), jnp.float32, least / len(pieces), high / len(pieces))
        gain = gain * jnp.repeat(jnp.exp(steps), extent[position] // parts).reshape((-1,) + (1,) * (len(extent) - 1 - position))
    return gain


def normal_values(rng, extent, spread, most, cuts=(), kind=jnp.bfloat16):
    level = block_scale(rng, extent, cuts, -0.22, 0.18) if cuts else 1.0
    values = jax.random.normal(rng, extent, jnp.float32) * spread * level
    return jnp.minimum(jnp.maximum(values, -most), most).astype(kind)


def setup_inputs(seed: int = 0) -> dict:
    splits = jax.random.split(jax.random.key(seed), 8)
    patches = normal_values(splits[0], (IMAGES, PATCHES, D), 1.0, 6.0, ((0, 128), (2, 4)))
    router = normal_values(splits[1], (D, EXPERTS), D ** -0.5, 0.15625, ((0, 4),))
    logits = draw_logits(jax.random.fold_in(splits[7], 71), 0)
    slot_outputs = normal_values(splits[3], (IMAGES, EXPERTS, D), 1.0, 6.0, ((0, 128), (2, 4)))
    cotangent = normal_values(splits[4], (IMAGES, PATCHES, D), 1.0, 6.0, ((0, 128), (2, 4)))
    weight_in = normal_values(splits[5], (EXPERTS, D, FF), D ** -0.5, 0.15625, ((0, 32), (2, 16)))
    weight_out = normal_values(splits[6], (EXPERTS, FF, D), FF ** -0.5, 0.078125, ((0, 32), (1, 16)))
    return {"patches": patches, "router": router, "logits": logits, "slot_outputs": slot_outputs, "cotangent": cotangent, "weight_in": weight_in, "weight_out": weight_out}


def softmax_backward(probs, upstream, axis):
    return probs * (upstream - lax.optimization_barrier(jnp.sum(probs * upstream, axis=axis, keepdims=True)))

def image_slots(items):
    logit_rows, patch_rows, grad_rows = items
    dispatch = jax.nn.softmax(logit_rows, axis=1)
    combine = jax.nn.softmax(logit_rows, axis=0)
    slot_inputs = jnp.dot(dispatch.astype(jnp.bfloat16), patch_rows, preferred_element_type=jnp.float32)
    slot_grads = jnp.dot(combine.astype(jnp.bfloat16), grad_rows, preferred_element_type=jnp.float32)
    return (slot_inputs.astype(jnp.bfloat16), slot_grads.astype(jnp.bfloat16))

def expert_backward(items):
    rows, grads, first, second = items
    before = jnp.dot(rows, first, preferred_element_type=jnp.float32)
    after, gelu_back = jax.vjp(jax.nn.gelu, before)
    after_low = after.astype(jnp.bfloat16)
    grad_after = jnp.dot(grads, second.T, preferred_element_type=jnp.float32)
    grad_second = jnp.dot(after_low.T, grads, preferred_element_type=jnp.float32).astype(jnp.bfloat16)
    grad_before = gelu_back(grad_after)[0].astype(jnp.bfloat16)
    grad_first = jnp.dot(rows.T, grad_before, preferred_element_type=jnp.float32).astype(jnp.bfloat16)
    returned = jnp.dot(grad_before, first.T, preferred_element_type=jnp.float32).astype(jnp.bfloat16)
    return (returned, grad_first, grad_second)

def image_backward(items):
    logit_rows, patch_rows, grad_rows, saved_rows, back_rows, router = items
    dispatch = jax.nn.softmax(logit_rows, axis=1)
    combine = jax.nn.softmax(logit_rows, axis=0)
    grad_dispatch = jnp.dot(back_rows, patch_rows.T, preferred_element_type=jnp.float32)
    grad_combine = jnp.dot(saved_rows, grad_rows.T, preferred_element_type=jnp.float32)
    grad_logits = softmax_backward(dispatch, grad_dispatch, 1) + softmax_backward(combine, grad_combine, 0)
    logit_low = grad_logits.astype(jnp.bfloat16)
    grad_patch = jnp.dot(dispatch.astype(jnp.bfloat16).T, back_rows, preferred_element_type=jnp.float32)
    grad_patch = grad_patch + jnp.dot(logit_low.T, router.T, preferred_element_type=jnp.float32)
    router_term = jnp.dot(patch_rows.T, logit_low.T, preferred_element_type=jnp.float32)
    return (grad_patch.astype(jnp.bfloat16), router_term)

def reference(patches, router, logits, slot_outputs, cotangent, weight_in, weight_out):
    slot_inputs, slot_grads = lax.map(image_slots, (logits, patches, cotangent))
    returned, grad_in, grad_out = lax.map(expert_backward, (jnp.transpose(slot_inputs, (1, 0, 2)), jnp.transpose(slot_grads, (1, 0, 2)), weight_in, weight_out))
    slot_back = jnp.transpose(returned, (1, 0, 2))

    def one_image(items):
        return image_backward(items + (router,))
    grad_patches, router_terms = lax.map(one_image, (logits, patches, cotangent, slot_outputs, slot_back))
    grad_router = lax.optimization_barrier(jnp.sum(router_terms, axis=0))
    return (grad_patches, grad_router, grad_in, grad_out)
```

```python
import jax
import jax.numpy as jnp
from jax import lax
from jax.experimental import pallas as pl
from jax.experimental.pallas import tpu as pltpu
from jax.sharding import Mesh
from jax.sharding import PartitionSpec as P

F32 = jnp.float32
BF16 = jnp.bfloat16
RING = ("zh", "tensor")
PLANE = ("dp", "y", "core")
COLUMN = ("y", "core")
CROSS = ("dp", "zh")


def call(kernel, outs, *args):
    return pl.pallas_call(
        kernel,
        out_shape=outs,
        compiler_params=pltpu.CompilerParams(vmem_limit_bytes=48 * 1024 * 1024),
    )(*args)


def shape(dims, dtype):
    return jax.ShapeDtypeStruct(dims, dtype)


def pieces():
    return [(8 * zh + 2 * y, 8 * y + 2 * zh) for zh in range(4) for y in range(4)]


def rounded_dot(a, b, dims):
    return lax.dot_general(a, b, (dims, ((), ())), preferred_element_type=F32)


def image_kernel(logits, patches, cotangent, saved, send, dispatch, combine, grad_combine):
    for new, old in pieces():
        dispatch[new : new + 2, :] = logits[0, old : old + 2, :]
    values = dispatch[...]
    top = jnp.exp(values - jnp.max(values, axis=1, keepdims=True))
    by_patch = top / jnp.sum(top, axis=1, keepdims=True)
    low = jnp.exp(values - jnp.max(values, axis=0, keepdims=True))
    by_slot = low / jnp.sum(low, axis=0, keepdims=True)
    dispatch[...] = by_patch
    combine[...] = by_slot
    slot_in = jnp.dot(by_patch.astype(BF16), patches[0], preferred_element_type=F32)
    slot_grad = jnp.dot(by_slot.astype(BF16), cotangent[0], preferred_element_type=F32)
    width = slot_in.shape[1]
    for zh in range(4):
        ins = slot_in[8 * zh : 8 * zh + 8, :].astype(BF16)
        grads = slot_grad[8 * zh : 8 * zh + 8, :].astype(BF16)
        for zl in range(4):
            send[4 * zh + zl, :, 0:width] = ins
            send[4 * zh + zl, :, width : 2 * width] = grads
    part = rounded_dot(saved[0], cotangent[0], ((1,), (1,)))
    for new, old in pieces():
        grad_combine[new : new + 2, :] = part[old : old + 2, :]


def regroup_kernel(got, send, stage):
    width = got.shape[2] // 2
    for zh in range(4):
        for zl in range(4):
            block = got[4 * zh + zl].astype(F32)
            for kind in range(2):
                row = 32 * kind + 8 * zh
                stage[row : row + 8, width * zl : width * (zl + 1)] = block[
                    :, width * kind : width * (kind + 1)
                ]
    row = lax.broadcasted_iota(jnp.int32, (64, 64), 0)
    col = lax.broadcasted_iota(jnp.int32, (64, 64), 1)
    move = (row == (col % 8) * 8 + col // 8).astype(F32).astype(BF16)
    moved = jnp.dot(move, stage[...].astype(BF16), preferred_element_type=F32).astype(BF16)
    for x in range(4):
        send[8 * x : 8 * x + 8] = moved.reshape(8, 8, 4 * width)


GELU_SCALE = 0.7978845608028654
GELU_CUBE = 0.044715


def expert_kernel(rows, first, second, send, grad_before, after):
    both = rows[...].reshape(256, rows.shape[2])
    before = jnp.dot(both, first[0], preferred_element_type=F32)
    grad_after = rounded_dot(both, second[0], ((1,), (1,)))
    grad_after = pltpu.roll(grad_after, 252, 0)
    is_in = lax.broadcasted_iota(jnp.int32, before.shape, 0) % 8 < 4
    square = before * before
    bent = jnp.tanh(GELU_SCALE * (before + GELU_CUBE * (before * square)))
    half = 0.5 * (1.0 + bent)
    slope = half + before * (
        (0.5 * GELU_SCALE) * ((1.0 - bent) * (1.0 + bent)) * (1.0 + (3.0 * GELU_CUBE) * square)
    )
    grads = jnp.where(is_in, grad_after * slope, 0.0)
    low = grads.astype(BF16)
    shifted = pltpu.roll(grads, 4, 0).astype(BF16)
    part = first.shape[1] // 2
    total = rounded_dot(low, first[0, :part, :], ((1,), (1,)))
    total = total + rounded_dot(shifted, first[0, part:, :], ((1,), (1,)))
    send[...] = total.astype(BF16).reshape(send.shape)
    grad_before[...] = low
    after[...] = pltpu.roll(jnp.where(is_in, before * half, 0.0), 4, 0).astype(BF16)


def weight_kernel(rows, grad_before, after, grad_first, grad_second):
    both = rows[...].reshape(256, rows.shape[2])
    grad_first[0] = rounded_dot(both, grad_before[...], ((0,), (0,))).astype(BF16)
    grad_second[0] = rounded_dot(after[...], both, ((0,), (0,))).astype(BF16)


def partial_kernel(got, send):
    total = got[0:8].astype(F32)
    for x in range(1, 4):
        total = total + got[8 * x : 8 * x + 8].astype(F32)
    low = total.reshape(64, got.shape[2]).astype(BF16)
    row = lax.broadcasted_iota(jnp.int32, (64, 64), 0)
    col = lax.broadcasted_iota(jnp.int32, (64, 64), 1)
    move = (row == (col % 8) * 8 + col // 8).astype(F32).astype(BF16)
    moved = jnp.dot(move, low, preferred_element_type=F32).astype(BF16)
    width = send.shape[2]
    for zh in range(4):
        for zl in range(4):
            at = (zl // 2) * 32 + 8 * zh
            lane = (zl % 2) * width
            send[4 * zh + zl] = moved[at : at + 8, lane : lane + width]


def back_kernel(got, patches, grad_combine, send, slot_back):
    for zh in range(4):
        total = got[4 * zh].astype(F32)
        for zl in range(1, 4):
            total = total + got[4 * zh + zl].astype(F32)
        slot_back[8 * zh : 8 * zh + 8, :] = total
    low = slot_back[...].astype(BF16)
    part = rounded_dot(low, patches[0], ((1,), (1,)))
    both = jnp.concatenate([part, grad_combine[...]], axis=0).astype(BF16)
    for zl in range(4):
        send[zl] = both


def logit_kernel(got, dispatch, combine, patches, grad_logits, send):
    total = got[0].astype(F32)
    for zl in range(1, 4):
        total = total + got[zl].astype(F32)
    by_patch, by_slot = dispatch[...], combine[...]
    up, down = total[:32], total[32:]
    grads = by_patch * (up - jnp.sum(by_patch * up, axis=1, keepdims=True))
    grads = grads + by_slot * (down - jnp.sum(by_slot * down, axis=0, keepdims=True))
    low = grads.astype(BF16)
    grad_logits[...] = low
    router = jnp.dot(low, patches[0], preferred_element_type=F32)
    width = send.shape[2]
    for j in range(8):
        lane = (j // 4) * width
        send[j] = router[(j % 4) * 8 : (j % 4) * 8 + 8, lane : lane + width]


def patch_kernel(dispatch, slot_back, grad_logits, router, grad_patches):
    new = lax.broadcasted_iota(jnp.int32, (32, 32), 0)
    old = lax.broadcasted_iota(jnp.int32, (32, 32), 1)
    move = (old == ((new // 2) % 4) * 8 + (new // 8) * 2 + new % 2).astype(F32).astype(BF16)
    columns = rounded_dot(move, router[...], ((1,), (1,))).astype(BF16)
    left = jnp.concatenate([dispatch[...], grad_logits[...].astype(F32)], axis=0).astype(BF16)
    right = jnp.concatenate([slot_back[...], columns.astype(F32)], axis=0).astype(BF16)
    grad_patches[0] = rounded_dot(left, right, ((0,), (0,))).astype(BF16)


def exchange(value, axes):
    return lax.all_to_all(value, axes, 0, 0, tiled=True)


def summed(value, axes, count):
    copies = jnp.broadcast_to(value[None], (count,) + value.shape)
    return jnp.sum(exchange(copies, axes), axis=0)


def body(patches, router, logits, slot_outputs, cotangent, weight_in, weight_out):
    count, width = patches.shape[1:]
    deep = weight_in.shape[1]
    hidden = weight_in.shape[2]
    send, dispatch, combine, grad_combine = call(
        image_kernel,
        [
            shape((16, 8, 2 * width), BF16),
            shape((32, count), F32),
            shape((32, count), F32),
            shape((32, count), F32),
        ],
        logits,
        patches,
        cotangent,
        slot_outputs,
    )
    got = exchange(send, RING)
    send = pl.pallas_call(
        regroup_kernel,
        out_shape=shape((32, 8, deep), BF16),
        scratch_shapes=[pltpu.VMEM((64, deep), F32)],
    )(got)
    rows = exchange(send, PLANE)
    send, grad_before, after = call(
        expert_kernel,
        [
            shape((32, 8, deep // 2), BF16),
            shape((256, hidden), BF16),
            shape((256, hidden), BF16),
        ],
        rows,
        weight_in,
        weight_out,
    )
    got = exchange(send, PLANE)
    grad_first, grad_second = call(
        weight_kernel,
        [shape((1, deep, hidden), BF16), shape((1, hidden, deep), BF16)],
        rows,
        grad_before,
        after,
    )
    send = call(partial_kernel, shape((16, 8, width), BF16), got)
    got = exchange(send, RING)
    send, slot_back = call(
        back_kernel,
        [shape((4, 64, count), BF16), shape((32, width), F32)],
        got,
        patches,
        grad_combine,
    )
    got = exchange(send, "tensor")
    grad_logits, send = call(
        logit_kernel,
        [shape((32, count), BF16), shape((8, 8, width // 2), F32)],
        got,
        dispatch,
        combine,
        patches,
    )
    own = jnp.sum(exchange(send, COLUMN), axis=0)
    grad_patches = call(
        patch_kernel,
        shape((1, count, width), BF16),
        dispatch,
        slot_back,
        grad_logits,
        router,
    )
    own = summed(own, CROSS, 16)
    whole = exchange(jnp.broadcast_to(own[None], (8,) + own.shape), COLUMN)
    whole = whole.reshape(2, 4, 4, 2, width // 2)
    grad_router = jnp.transpose(whole, (0, 4, 2, 1, 3)).reshape(width, 32)
    return (grad_patches, grad_router, grad_first, grad_second)


def solution(mesh):
    split = Mesh(mesh.devices.reshape(4, 4, 4, 2, 4), ("dp", "y", "zh", "core", "tensor"))
    images = ("dp", "y", "zh", "core")
    experts = ("y", "zh", "core")
    return jax.shard_map(
        body,
        mesh=split,
        in_specs=(
            P(images, None, "tensor"),
            P("tensor", None),
            P(images, None, None),
            P(images, None, "tensor"),
            P(images, None, "tensor"),
            P(experts, None, ("dp", "tensor")),
            P(experts, ("dp", "tensor"), None),
        ),
        out_specs=(
            P(images, None, "tensor"),
            P("tensor", None),
            P(experts, None, ("dp", "tensor")),
            P(experts, ("dp", "tensor"), None),
        ),
        check_vma=False,
    )
```

```python
import jax
import jax.numpy as jnp
from jax import lax
from jax.experimental import pallas as pl
from jax.experimental.pallas import tpu as pltpu
from jax.sharding import Mesh
from jax.sharding import PartitionSpec as P

F32 = jnp.float32
BF16 = jnp.bfloat16
RING = ("zh", "tensor")
PLANE = ("dp", "y", "core")
SHEET = ("dp", "y")
LINE = ("zh", "core")


def call(kernel, outs, *args, scratch=()):
    return pl.pallas_call(
        kernel,
        out_shape=outs,
        scratch_shapes=scratch,
        compiler_params=pltpu.CompilerParams(vmem_limit_bytes=24 * 1024 * 1024),
    )(*args)


def shape(dims, dtype):
    return jax.ShapeDtypeStruct(dims, dtype)


def pieces():
    return [(8 * zh + 2 * y, 8 * y + 2 * zh) for zh in range(4) for y in range(4)]


def rounded_dot(a, b, dims):
    return lax.dot_general(a, b, (dims, ((), ())), preferred_element_type=F32)


def image_kernel(far_logits, far_patches, far_cotangent, far_saved, send, dispatch, combine_term, *scratch):
    logits, patches, cotangent, saved, stage, arrived = scratch
    copies = [
        pltpu.make_async_copy(source, target, arrived.at[i])
        for i, (source, target) in enumerate(
            [
                (far_logits, logits),
                (far_patches, patches),
                (far_cotangent, cotangent),
                (far_saved, saved),
            ]
        )
    ]
    for copy in copies:
        copy.start()
    copies[0].wait()
    for new, old in pieces():
        dispatch[new : new + 2, :] = logits[0, old : old + 2, :]
    values = dispatch[...]
    top = jnp.exp(values - jnp.max(values, axis=1, keepdims=True))
    by_patch = top / jnp.sum(top, axis=1, keepdims=True)
    low = jnp.exp(values - jnp.max(values, axis=0, keepdims=True))
    by_slot = low / jnp.sum(low, axis=0, keepdims=True)
    dispatch[...] = by_patch
    copies[1].wait()
    slot_in = rounded_dot(by_patch.astype(BF16), patches[0], ((1,), (1,)))
    copies[2].wait()
    slot_grad = rounded_dot(by_slot.astype(BF16), cotangent[0], ((1,), (1,)))
    width = slot_in.shape[1]
    for zh in range(4):
        ins = slot_in[8 * zh : 8 * zh + 8, :].astype(BF16)
        grads = slot_grad[8 * zh : 8 * zh + 8, :].astype(BF16)
        for zl in range(4):
            send[4 * zh + zl, :, 0:width] = ins
            send[4 * zh + zl, :, width : 2 * width] = grads
    copies[3].wait()
    part = jnp.dot(saved[0], cotangent[0], preferred_element_type=F32)
    for new, old in pieces():
        stage[new : new + 2, :] = part[old : old + 2, :]
    part = stage[...]
    combine_term[...] = by_slot * (part - jnp.sum(by_slot * part, axis=0, keepdims=True))


def regroup_kernel(got, send, stage):
    width = got.shape[2] // 2
    for zh in range(4):
        for zl in range(4):
            block = got[4 * zh + zl].astype(F32)
            for kind in range(2):
                row = 32 * kind + 8 * zh
                stage[row : row + 8, width * zl : width * (zl + 1)] = block[
                    :, width * kind : width * (kind + 1)
                ]
    row = lax.broadcasted_iota(jnp.int32, (64, 64), 0)
    col = lax.broadcasted_iota(jnp.int32, (64, 64), 1)
    move = (row == (col % 8) * 8 + col // 8).astype(F32).astype(BF16)
    moved = jnp.dot(move, stage[...].astype(BF16), preferred_element_type=F32).astype(BF16)
    for x in range(4):
        send[8 * x : 8 * x + 8] = moved.reshape(8, 8, 4 * width)


GELU_SCALE = 0.7978845608028654
GELU_CUBE = 0.044715


def expert_kernel(rows, first, second, send, grad_before, after):
    both = rows[...].reshape(256, rows.shape[2])
    before = rounded_dot(both, first[0], ((1,), (1,)))
    grad_after = rounded_dot(both, second[0], ((1,), (1,)))
    grad_after = pltpu.roll(grad_after, 252, 0)
    is_in = lax.broadcasted_iota(jnp.int32, before.shape, 0) % 8 < 4
    square = before * before
    bent = jnp.tanh(GELU_SCALE * (before + GELU_CUBE * (before * square)))
    half = 0.5 * (1.0 + bent)
    slope = half + before * (
        (0.5 * GELU_SCALE) * ((1.0 - bent) * (1.0 + bent)) * (1.0 + (3.0 * GELU_CUBE) * square)
    )
    grads = jnp.where(is_in, grad_after * slope, 0.0)
    low = grads.astype(BF16)
    shifted = pltpu.roll(grads, 4, 0).astype(BF16)
    part = first.shape[2] // 2
    total = jnp.dot(low, first[0, :, :part], preferred_element_type=F32)
    total = total + jnp.dot(shifted, first[0, :, part:], preferred_element_type=F32)
    send[...] = total.astype(BF16).reshape(send.shape)
    grad_before[...] = low
    after[...] = pltpu.roll(jnp.where(is_in, before * half, 0.0), 4, 0).astype(BF16)


def weight_kernel(rows, grad_before, after, grad_first, grad_second):
    both = rows[...].reshape(256, rows.shape[2])
    grad_first[0] = rounded_dot(grad_before[...], both, ((0,), (0,))).astype(BF16)
    grad_second[0] = rounded_dot(after[...], both, ((0,), (0,))).astype(BF16)


def partial_kernel(got, send):
    total = got[0:8].astype(F32)
    for x in range(1, 4):
        total = total + got[8 * x : 8 * x + 8].astype(F32)
    low = total.reshape(64, got.shape[2]).astype(BF16)
    row = lax.broadcasted_iota(jnp.int32, (64, 64), 0)
    col = lax.broadcasted_iota(jnp.int32, (64, 64), 1)
    move = (row == (col % 8) * 8 + col // 8).astype(F32).astype(BF16)
    moved = jnp.dot(move, low, preferred_element_type=F32).astype(BF16)
    width = send.shape[2]
    for zh in range(4):
        for zl in range(4):
            at = (zl // 2) * 32 + 8 * zh
            lane = (zl % 2) * width
            send[4 * zh + zl] = moved[at : at + 8, lane : lane + width]


def back_kernel(got, patches, dispatch, combine_term, send, slot_back):
    for zh in range(4):
        total = got[4 * zh].astype(F32)
        for zl in range(1, 4):
            total = total + got[4 * zh + zl].astype(F32)
        slot_back[8 * zh : 8 * zh + 8, :] = total
    low = slot_back[...].astype(BF16)
    part = jnp.dot(low, patches[0], preferred_element_type=F32)
    by_patch = dispatch[...]
    grads = by_patch * (part - jnp.sum(by_patch * part, axis=1, keepdims=True))
    grads = (grads + combine_term[...]).astype(BF16)
    for zl in range(4):
        send[zl] = grads


def logit_kernel(got, patches, grad_logits, send, stage):
    total = got[0].astype(F32)
    for zl in range(1, 4):
        total = total + got[zl].astype(F32)
    low = total.astype(BF16)
    grad_logits[...] = low
    router = rounded_dot(low, patches[0], ((1,), (1,)))
    for new, old in pieces():
        stage[old : old + 2, :] = router[new : new + 2, :]
    router = stage[...].astype(BF16)
    for j in range(16):
        send[j] = router


def patch_kernel(dispatch, slot_back, grad_logits, router, grad_patches):
    new = lax.broadcasted_iota(jnp.int32, (32, 32), 0)
    old = lax.broadcasted_iota(jnp.int32, (32, 32), 1)
    move = (old == ((new // 2) % 4) * 8 + (new // 8) * 2 + new % 2).astype(F32).astype(BF16)
    columns = jnp.dot(move, router[...], preferred_element_type=F32)
    left = jnp.concatenate([dispatch[...], grad_logits[...].astype(F32)], axis=0).astype(BF16)
    right = jnp.concatenate([slot_back[...], columns], axis=0).astype(BF16)
    grad_patches[0] = rounded_dot(right, left, ((0,), (0,))).astype(BF16)


def add_kernel(got, send):
    total = got[0].astype(F32)
    for j in range(1, 16):
        total = total + got[j].astype(F32)
    low = total.astype(BF16)
    for j in range(8):
        send[j] = low


def total_kernel(got, grad_router):
    total = got[0].astype(F32)
    for j in range(1, 8):
        total = total + got[j].astype(F32)
    grad_router[...] = total


def exchange(value, axes):
    return lax.all_to_all(value, axes, 0, 0, tiled=True)


def body(patches, router, logits, slot_outputs, cotangent, weight_in, weight_out):
    count, width = patches.shape[1:]
    deep = weight_in.shape[1]
    hidden = weight_in.shape[2]
    patches = jnp.swapaxes(patches, 1, 2)
    cotangent = jnp.swapaxes(cotangent, 1, 2)
    send, dispatch, combine_term = pl.pallas_call(
        image_kernel,
        in_specs=[pl.BlockSpec(memory_space=pltpu.HBM)] * 4,
        scratch_shapes=[
            pltpu.VMEM(logits.shape, F32),
            pltpu.VMEM(patches.shape, BF16),
            pltpu.VMEM(cotangent.shape, BF16),
            pltpu.VMEM(slot_outputs.shape, BF16),
            pltpu.VMEM((32, count), F32),
            pltpu.SemaphoreType.DMA((4,)),
        ],
        compiler_params=pltpu.CompilerParams(vmem_limit_bytes=60 * 1024 * 1024),
        out_shape=[
            shape((16, 8, 2 * width), BF16),
            shape((32, count), F32),
            shape((32, count), F32),
        ],
    )(logits, patches, cotangent, slot_outputs)
    got = exchange(send, RING)
    send = call(
        regroup_kernel,
        shape((32, 8, deep), BF16),
        got,
        scratch=[pltpu.VMEM((64, deep), F32)],
    )
    rows = exchange(send, PLANE)
    send, grad_before, after = call(
        expert_kernel,
        [
            shape((32, 8, deep // 2), BF16),
            shape((256, hidden), BF16),
            shape((256, hidden), BF16),
        ],
        rows,
        jnp.swapaxes(weight_in, 1, 2),
        weight_out,
    )
    got = exchange(send, PLANE)
    grad_first, grad_second = call(
        weight_kernel,
        [shape((1, hidden, deep), BF16), shape((1, hidden, deep), BF16)],
        rows,
        grad_before,
        after,
    )
    send = call(partial_kernel, shape((16, 8, width), BF16), got)
    got = exchange(send, RING)
    send, slot_back = call(
        back_kernel,
        [shape((4, 32, count), BF16), shape((32, width), F32)],
        got,
        patches,
        dispatch,
        combine_term,
    )
    got = exchange(send, "tensor")
    grad_logits, send = call(
        logit_kernel,
        [shape((32, count), BF16), shape((16, 32, width), BF16)],
        got,
        patches,
        scratch=[pltpu.VMEM((32, width), F32)],
    )
    got = exchange(send, SHEET)
    grad_patches = call(
        patch_kernel,
        shape((1, width, count), BF16),
        dispatch,
        slot_back,
        grad_logits,
        jnp.swapaxes(router, 0, 1),
    )
    got = exchange(call(add_kernel, shape((8, 32, width), BF16), got), LINE)
    grad_router = call(total_kernel, shape((32, width), F32), got)
    return (
        jnp.swapaxes(grad_patches, 1, 2),
        jnp.swapaxes(grad_router, 0, 1),
        jnp.swapaxes(grad_first, 1, 2),
        grad_second,
    )


def solution(mesh):
    split = Mesh(mesh.devices.reshape(4, 4, 4, 2, 4), ("dp", "y", "zh", "core", "tensor"))
    images = ("dp", "y", "zh", "core")
    experts = ("y", "zh", "core")
    return jax.shard_map(
        body,
        mesh=split,
        in_specs=(
            P(images, None, "tensor"),
            P("tensor", None),
            P(images, None, None),
            P(images, None, "tensor"),
            P(images, None, "tensor"),
            P(experts, None, ("dp", "tensor")),
            P(experts, ("dp", "tensor"), None),
        ),
        out_specs=(
            P(images, None, "tensor"),
            P("tensor", None),
            P(experts, None, ("dp", "tensor")),
            P(experts, ("dp", "tensor"), None),
        ),
        check_vma=False,
    )
```

```python
import jax
import jax.numpy as jnp
from jax import lax
from jax.experimental import pallas as pl
from jax.experimental.pallas import tpu as pltpu
from jax.sharding import Mesh
from jax.sharding import PartitionSpec as P

F32 = jnp.float32
BF16 = jnp.bfloat16
RING = ("zh", "tensor")
PLANE = ("dp", "y", "core")


def call(kernel, outs, *args, scratch=()):
    return pl.pallas_call(
        kernel,
        out_shape=outs,
        scratch_shapes=scratch,
        compiler_params=pltpu.CompilerParams(vmem_limit_bytes=24 * 1024 * 1024),
    )(*args)


def shape(dims, dtype):
    return jax.ShapeDtypeStruct(dims, dtype)


def pieces():
    return [(8 * zh + 2 * y, 8 * y + 2 * zh) for zh in range(4) for y in range(4)]


def rounded_dot(a, b, dims):
    return lax.dot_general(a, b, (dims, ((), ())), preferred_element_type=F32)


def soft(values, axis):
    top = jnp.exp(values - jnp.max(values, axis=axis, keepdims=True))
    return top / jnp.sum(top, axis=axis, keepdims=True)


def image_kernel(far_logits, far_patches, far_cotangent, send, dispatch, *scratch):
    logits, patches, cotangent, arrived = scratch
    copies = [
        pltpu.make_async_copy(source, target, arrived.at[i])
        for i, (source, target) in enumerate(
            [(far_logits, logits), (far_patches, patches), (far_cotangent, cotangent)]
        )
    ]
    for copy in copies:
        copy.start()
    copies[0].wait()
    for new, old in pieces():
        dispatch[new : new + 2, :] = logits[0, old : old + 2, :]
    values = dispatch[...]
    by_patch = soft(values, 1)
    by_slot = soft(values, 0)
    dispatch[...] = by_patch
    copies[1].wait()
    slot_in = rounded_dot(by_patch.astype(BF16), patches[0], ((1,), (1,)))
    copies[2].wait()
    slot_grad = rounded_dot(by_slot.astype(BF16), cotangent[0], ((1,), (1,)))
    width = slot_in.shape[1]
    for zh in range(4):
        ins = slot_in[8 * zh : 8 * zh + 8, :].astype(BF16)
        grads = slot_grad[8 * zh : 8 * zh + 8, :].astype(BF16)
        for zl in range(4):
            send[4 * zh + zl, :, 0:width] = ins
            send[4 * zh + zl, :, width : 2 * width] = grads


def combine_kernel(logits, cotangent, saved, combine_term):
    by_slot = soft(logits[0], 0)
    part = jnp.dot(saved[0], cotangent[0], preferred_element_type=F32)
    term = by_slot * (part - jnp.sum(by_slot * part, axis=0, keepdims=True))
    for new, old in pieces():
        combine_term[new : new + 2, :] = term[old : old + 2, :]


def regroup_kernel(got, send, stage):
    width = got.shape[2] // 2
    for zh in range(4):
        for zl in range(4):
            block = got[4 * zh + zl].astype(F32)
            for kind in range(2):
                row = 32 * kind + 8 * zh
                stage[row : row + 8, width * zl : width * (zl + 1)] = block[
                    :, width * kind : width * (kind + 1)
                ]
    row = lax.broadcasted_iota(jnp.int32, (64, 64), 0)
    col = lax.broadcasted_iota(jnp.int32, (64, 64), 1)
    move = (row == (col % 8) * 8 + col // 8).astype(F32).astype(BF16)
    moved = jnp.dot(move, stage[...].astype(BF16), preferred_element_type=F32).astype(BF16)
    for x in range(4):
        send[8 * x : 8 * x + 8] = moved.reshape(8, 8, 4 * width)


GELU_SCALE = 0.7978845608028654
GELU_CUBE = 0.044715


def expert_kernel(rows, first, second, send, grad_before, after):
    both = rows[...].reshape(256, rows.shape[2])
    before = rounded_dot(both, first[0], ((1,), (1,)))
    grad_after = rounded_dot(both, second[0], ((1,), (1,)))
    grad_after = pltpu.roll(grad_after, 252, 0)
    is_in = lax.broadcasted_iota(jnp.int32, before.shape, 0) % 8 < 4
    square = before * before
    bent = jnp.tanh(GELU_SCALE * (before + GELU_CUBE * (before * square)))
    half = 0.5 * (1.0 + bent)
    slope = half + before * (
        (0.5 * GELU_SCALE) * ((1.0 - bent) * (1.0 + bent)) * (1.0 + (3.0 * GELU_CUBE) * square)
    )
    grads = jnp.where(is_in, grad_after * slope, 0.0)
    low = grads.astype(BF16)
    shifted = pltpu.roll(grads, 4, 0).astype(BF16)
    part = first.shape[2] // 2
    total = jnp.dot(low, first[0, :, :part], preferred_element_type=F32)
    total = total + jnp.dot(shifted, first[0, :, part:], preferred_element_type=F32)
    send[...] = total.astype(BF16).reshape(send.shape)
    grad_before[...] = low
    after[...] = pltpu.roll(jnp.where(is_in, before * half, 0.0), 4, 0).astype(BF16)


def weight_kernel(rows, grad_before, after, grad_first, grad_second):
    both = rows[...].reshape(256, rows.shape[2])
    grad_first[0] = rounded_dot(grad_before[...], both, ((0,), (0,))).astype(BF16)
    grad_second[0] = rounded_dot(after[...], both, ((0,), (0,))).astype(BF16)


def partial_kernel(got, send):
    total = got[0:8].astype(F32)
    for x in range(1, 4):
        total = total + got[8 * x : 8 * x + 8].astype(F32)
    low = total.reshape(64, got.shape[2]).astype(BF16)
    row = lax.broadcasted_iota(jnp.int32, (64, 64), 0)
    col = lax.broadcasted_iota(jnp.int32, (64, 64), 1)
    move = (row == (col % 8) * 8 + col // 8).astype(F32).astype(BF16)
    moved = jnp.dot(move, low, preferred_element_type=F32).astype(BF16)
    width = send.shape[2]
    for zh in range(4):
        for zl in range(4):
            at = (zl // 2) * 32 + 8 * zh
            lane = (zl % 2) * width
            send[4 * zh + zl] = moved[at : at + 8, lane : lane + width]


def back_kernel(got, patches, dispatch, combine_term, send, slot_back):
    for zh in range(4):
        total = got[4 * zh].astype(F32)
        for zl in range(1, 4):
            total = total + got[4 * zh + zl].astype(F32)
        slot_back[8 * zh : 8 * zh + 8, :] = total
    low = slot_back[...].astype(BF16)
    part = jnp.dot(low, patches[0], preferred_element_type=F32)
    by_patch = dispatch[...]
    grads = by_patch * (part - jnp.sum(by_patch * part, axis=1, keepdims=True))
    grads = (grads + combine_term[...]).astype(BF16)
    for zl in range(4):
        send[zl] = grads


def logit_kernel(got, patches, grad_logits, send, stage):
    total = got[0].astype(F32)
    for zl in range(1, 4):
        total = total + got[zl].astype(F32)
    low = total.astype(BF16)
    grad_logits[...] = low
    router = rounded_dot(low, patches[0], ((1,), (1,)))
    for new, old in pieces():
        stage[old : old + 2, :] = router[new : new + 2, :]
    for core in range(2):
        at = 16 * core
        rows = stage[at : at + 16, :].astype(BF16)
        rest = jnp.concatenate([stage[at : at + 8, 256:], stage[at + 8 : at + 16, 256:]], axis=1)
        rest = rest.astype(BF16)
        for j in range(16):
            send[2 * j + core, 0:16, :] = rows[:, 0:128]
            send[2 * j + core, 16:32, :] = rows[:, 128:256]
            send[2 * j + core, 32:40, :] = rest


def patch_kernel(dispatch, slot_back, grad_logits, router, grad_patches):
    new = lax.broadcasted_iota(jnp.int32, (32, 32), 0)
    old = lax.broadcasted_iota(jnp.int32, (32, 32), 1)
    move = (old == ((new // 2) % 4) * 8 + (new // 8) * 2 + new % 2).astype(F32).astype(BF16)
    columns = jnp.dot(move, router[...], preferred_element_type=F32)
    left = jnp.concatenate([dispatch[...], grad_logits[...].astype(F32)], axis=0).astype(BF16)
    right = jnp.concatenate([slot_back[...], columns], axis=0).astype(BF16)
    grad_patches[0] = rounded_dot(right, left, ((0,), (0,))).astype(BF16)


def add_kernel(got, send):
    total = got[0].astype(F32)
    for j in range(1, got.shape[0]):
        total = total + got[j].astype(F32)
    total = total.astype(send.dtype)
    for j in range(send.shape[0]):
        send[j] = total


def total_kernel(got, grad_router):
    for core in range(2):
        at = 16 * core
        total = got[core].astype(F32)
        for zh in range(1, 4):
            total = total + got[2 * zh + core].astype(F32)
        grad_router[at : at + 16, 0:128] = total[0:16, :]
        grad_router[at : at + 16, 128:256] = total[16:32, :]
        grad_router[at : at + 8, 256:320] = total[32:40, 0:64]
        grad_router[at + 8 : at + 16, 256:320] = total[32:40, 64:128]


def exchange(value, axes):
    return lax.all_to_all(value, axes, 0, 0, tiled=True)


def body(patches, router, logits, slot_outputs, cotangent, weight_in, weight_out):
    count, width = patches.shape[1:]
    deep = weight_in.shape[1]
    hidden = weight_in.shape[2]
    patches = jnp.swapaxes(patches, 1, 2)
    cotangent = jnp.swapaxes(cotangent, 1, 2)
    send, dispatch = pl.pallas_call(
        image_kernel,
        in_specs=[pl.BlockSpec(memory_space=pltpu.HBM)] * 3,
        scratch_shapes=[
            pltpu.VMEM(logits.shape, F32),
            pltpu.VMEM(patches.shape, BF16),
            pltpu.VMEM(cotangent.shape, BF16),
            pltpu.SemaphoreType.DMA((3,)),
        ],
        compiler_params=pltpu.CompilerParams(vmem_limit_bytes=60 * 1024 * 1024),
        out_shape=[
            shape((16, 8, 2 * width), BF16),
            shape((32, count), F32),
        ],
    )(logits, patches, cotangent)
    combine_term = call(
        combine_kernel, shape((32, count), F32), logits, cotangent, slot_outputs
    )
    got, combine_term = lax.optimization_barrier((exchange(send, RING), combine_term))
    send = call(
        regroup_kernel,
        shape((32, 8, deep), BF16),
        got,
        scratch=[pltpu.VMEM((64, deep), F32)],
    )
    rows = exchange(send, PLANE)
    send, grad_before, after = call(
        expert_kernel,
        [
            shape((32, 8, deep // 2), BF16),
            shape((256, hidden), BF16),
            shape((256, hidden), BF16),
        ],
        rows,
        jnp.swapaxes(weight_in, 1, 2),
        weight_out,
    )
    got = exchange(send, PLANE)
    grad_first, grad_second = call(
        weight_kernel,
        [shape((1, hidden, deep), BF16), shape((1, hidden, deep), BF16)],
        rows,
        grad_before,
        after,
    )
    send = call(partial_kernel, shape((16, 8, width), BF16), got)
    got = exchange(send, RING)
    send, slot_back = call(
        back_kernel,
        [shape((4, 32, count), BF16), shape((32, width), F32)],
        got,
        patches,
        dispatch,
        combine_term,
    )
    got = exchange(send, "tensor")
    grad_logits, send = call(
        logit_kernel,
        [shape((32, count), BF16), shape((32, 40, 128), BF16)],
        got,
        patches,
        scratch=[pltpu.VMEM((32, width), F32)],
    )
    got = exchange(send, PLANE)
    grad_patches = call(
        patch_kernel,
        shape((1, width, count), BF16),
        dispatch,
        slot_back,
        grad_logits,
        jnp.swapaxes(router, 0, 1),
    )
    got = exchange(call(add_kernel, shape((8, 40, 128), BF16), got), ("zh", "core"))
    grad_router = call(total_kernel, shape((32, width), F32), got)
    return (
        jnp.swapaxes(grad_patches, 1, 2),
        jnp.swapaxes(grad_router, 0, 1),
        jnp.swapaxes(grad_first, 1, 2),
        grad_second,
    )


def solution(mesh):
    split = Mesh(mesh.devices.reshape(4, 4, 4, 2, 4), ("dp", "y", "zh", "core", "tensor"))
    images = ("dp", "y", "zh", "core")
    experts = ("y", "zh", "core")
    return jax.shard_map(
        body,
        mesh=split,
        in_specs=(
            P(images, None, "tensor"),
            P("tensor", None),
            P(images, None, None),
            P(images, None, "tensor"),
            P(images, None, "tensor"),
            P(experts, None, ("dp", "tensor")),
            P(experts, ("dp", "tensor"), None),
        ),
        out_specs=(
            P(images, None, "tensor"),
            P("tensor", None),
            P(experts, None, ("dp", "tensor")),
            P(experts, ("dp", "tensor"), None),
        ),
        check_vma=False,
    )
```

```python
import jax
import jax.numpy as jnp
from jax import lax
from jax.experimental import pallas as pl
from jax.experimental.pallas import tpu as pltpu
from jax.sharding import Mesh
from jax.sharding import PartitionSpec as P

F32 = jnp.float32
BF16 = jnp.bfloat16
RING = ("zh", "tensor")
PLANE = ("dp", "y", "core")


def call(kernel, outs, *args, scratch=()):
    return pl.pallas_call(
        kernel,
        out_shape=outs,
        scratch_shapes=scratch,
        compiler_params=pltpu.CompilerParams(vmem_limit_bytes=24 * 1024 * 1024),
    )(*args)


def shape(dims, dtype):
    return jax.ShapeDtypeStruct(dims, dtype)


def pieces():
    return [(8 * zh + 2 * y, 8 * y + 2 * zh) for zh in range(4) for y in range(4)]


def rounded_dot(a, b, dims):
    return lax.dot_general(a, b, (dims, ((), ())), preferred_element_type=F32)


def soft(values, axis):
    top = jnp.exp(values - jnp.max(values, axis=axis, keepdims=True))
    return top / jnp.sum(top, axis=axis, keepdims=True)


def image_kernel(far_logits, far_patches, far_cotangent, send, dispatch, *scratch):
    logits, patches, cotangent, arrived = scratch
    copies = [
        pltpu.make_async_copy(source, target, arrived.at[i])
        for i, (source, target) in enumerate(
            [(far_logits, logits), (far_patches, patches), (far_cotangent, cotangent)]
        )
    ]
    for copy in copies:
        copy.start()
    copies[0].wait()
    for new, old in pieces():
        dispatch[new : new + 2, :] = logits[0, old : old + 2, :]
    values = dispatch[...]
    by_patch = soft(values, 1)
    by_slot = soft(values, 0)
    dispatch[...] = by_patch
    copies[1].wait()
    slot_in = rounded_dot(by_patch.astype(BF16), patches[0], ((1,), (1,)))
    copies[2].wait()
    slot_grad = rounded_dot(by_slot.astype(BF16), cotangent[0], ((1,), (1,)))
    width = slot_in.shape[1]
    for zh in range(4):
        ins = slot_in[8 * zh : 8 * zh + 8, :].astype(BF16)
        grads = slot_grad[8 * zh : 8 * zh + 8, :].astype(BF16)
        for zl in range(4):
            send[4 * zh + zl, :, 0:width] = ins
            send[4 * zh + zl, :, width : 2 * width] = grads


def regroup_kernel(got, send, stage):
    width = got.shape[2] // 2
    for zh in range(4):
        for zl in range(4):
            block = got[4 * zh + zl].astype(F32)
            for kind in range(2):
                row = 32 * kind + 8 * zh
                stage[row : row + 8, width * zl : width * (zl + 1)] = block[
                    :, width * kind : width * (kind + 1)
                ]
    row = lax.broadcasted_iota(jnp.int32, (64, 64), 0)
    col = lax.broadcasted_iota(jnp.int32, (64, 64), 1)
    move = (row == (col % 8) * 8 + col // 8).astype(F32).astype(BF16)
    moved = jnp.dot(move, stage[...].astype(BF16), preferred_element_type=F32).astype(BF16)
    for x in range(4):
        send[8 * x : 8 * x + 8] = moved.reshape(8, 8, 4 * width)


GELU_SCALE = 0.7978845608028654
GELU_CUBE = 0.044715


def expert_kernel(
    rows, first, second, logits, cotangent, saved, send, grad_before, after, combine_term
):
    by_slot = soft(logits[0], 0)
    part = jnp.dot(saved[0], cotangent[0], preferred_element_type=F32)
    term = by_slot * (part - jnp.sum(by_slot * part, axis=0, keepdims=True))
    for new, old in pieces():
        combine_term[new : new + 2, :] = term[old : old + 2, :]
    both = rows[...].reshape(256, rows.shape[2])
    before = rounded_dot(both, first[0], ((1,), (1,)))
    grad_after = rounded_dot(both, second[0], ((1,), (1,)))
    grad_after = pltpu.roll(grad_after, 252, 0)
    is_in = lax.broadcasted_iota(jnp.int32, before.shape, 0) % 8 < 4
    square = before * before
    bent = jnp.tanh(GELU_SCALE * (before + GELU_CUBE * (before * square)))
    half = 0.5 * (1.0 + bent)
    slope = half + before * (
        (0.5 * GELU_SCALE) * ((1.0 - bent) * (1.0 + bent)) * (1.0 + (3.0 * GELU_CUBE) * square)
    )
    grads = jnp.where(is_in, grad_after * slope, 0.0)
    low = grads.astype(BF16)
    shifted = pltpu.roll(grads, 4, 0).astype(BF16)
    part = first.shape[2] // 2
    total = jnp.dot(low, first[0, :, :part], preferred_element_type=F32)
    total = total + jnp.dot(shifted, first[0, :, part:], preferred_element_type=F32)
    send[...] = total.astype(BF16).reshape(send.shape)
    grad_before[...] = low
    after[...] = pltpu.roll(jnp.where(is_in, before * half, 0.0), 4, 0).astype(BF16)


def weight_kernel(rows, grad_before, after, grad_first, grad_second):
    both = rows[...].reshape(256, rows.shape[2])
    grad_first[0] = rounded_dot(grad_before[...], both, ((0,), (0,))).astype(BF16)
    grad_second[0] = rounded_dot(after[...], both, ((0,), (0,))).astype(BF16)


def partial_kernel(got, send):
    total = got[0:8].astype(F32)
    for x in range(1, 4):
        total = total + got[8 * x : 8 * x + 8].astype(F32)
    low = total.reshape(64, got.shape[2]).astype(BF16)
    row = lax.broadcasted_iota(jnp.int32, (64, 64), 0)
    col = lax.broadcasted_iota(jnp.int32, (64, 64), 1)
    move = (row == (col % 8) * 8 + col // 8).astype(F32).astype(BF16)
    moved = jnp.dot(move, low, preferred_element_type=F32).astype(BF16)
    width = send.shape[2]
    for zh in range(4):
        for zl in range(4):
            at = (zl // 2) * 32 + 8 * zh
            lane = (zl % 2) * width
            send[4 * zh + zl] = moved[at : at + 8, lane : lane + width]


def back_kernel(got, patches, dispatch, combine_term, send, slot_back):
    for zh in range(4):
        total = got[4 * zh].astype(F32)
        for zl in range(1, 4):
            total = total + got[4 * zh + zl].astype(F32)
        slot_back[8 * zh : 8 * zh + 8, :] = total
    low = slot_back[...].astype(BF16)
    part = jnp.dot(low, patches[0], preferred_element_type=F32)
    by_patch = dispatch[...]
    grads = by_patch * (part - jnp.sum(by_patch * part, axis=1, keepdims=True))
    grads = (grads + combine_term[...]).astype(BF16)
    for zl in range(4):
        send[zl] = grads


def logit_kernel(got, patches, grad_logits, send, stage):
    total = got[0].astype(F32)
    for zl in range(1, 4):
        total = total + got[zl].astype(F32)
    low = total.astype(BF16)
    grad_logits[...] = low
    router = rounded_dot(low, patches[0], ((1,), (1,)))
    for new, old in pieces():
        stage[old : old + 2, :] = router[new : new + 2, :]
    for core in range(2):
        at = 16 * core
        rows = stage[at : at + 16, :].astype(BF16)
        rest = jnp.concatenate([stage[at : at + 8, 256:], stage[at + 8 : at + 16, 256:]], axis=1)
        rest = rest.astype(BF16)
        for j in range(16):
            send[2 * j + core, 0:16, :] = rows[:, 0:128]
            send[2 * j + core, 16:32, :] = rows[:, 128:256]
            send[2 * j + core, 32:40, :] = rest


def patch_kernel(dispatch, slot_back, grad_logits, router, grad_patches):
    new = lax.broadcasted_iota(jnp.int32, (32, 32), 0)
    old = lax.broadcasted_iota(jnp.int32, (32, 32), 1)
    move = (old == ((new // 2) % 4) * 8 + (new // 8) * 2 + new % 2).astype(F32).astype(BF16)
    columns = jnp.dot(move, router[...], preferred_element_type=F32)
    left = jnp.concatenate([dispatch[...], grad_logits[...].astype(F32)], axis=0).astype(BF16)
    right = jnp.concatenate([slot_back[...], columns], axis=0).astype(BF16)
    grad_patches[0] = rounded_dot(right, left, ((0,), (0,))).astype(BF16)


def add_kernel(got, send):
    total = got[0].astype(F32)
    for j in range(1, got.shape[0]):
        total = total + got[j].astype(F32)
    total = total.astype(send.dtype)
    for j in range(send.shape[0]):
        send[j] = total


def total_kernel(got, grad_router):
    for core in range(2):
        at = 16 * core
        total = got[core].astype(F32)
        for zh in range(1, 4):
            total = total + got[2 * zh + core].astype(F32)
        grad_router[at : at + 16, 0:128] = total[0:16, :]
        grad_router[at : at + 16, 128:256] = total[16:32, :]
        grad_router[at : at + 8, 256:320] = total[32:40, 0:64]
        grad_router[at + 8 : at + 16, 256:320] = total[32:40, 64:128]


def exchange(value, axes):
    return lax.all_to_all(value, axes, 0, 0, tiled=True)


def body(patches, router, logits, slot_outputs, cotangent, weight_in, weight_out):
    count, width = patches.shape[1:]
    deep = weight_in.shape[1]
    hidden = weight_in.shape[2]
    patches = jnp.swapaxes(patches, 1, 2)
    cotangent = jnp.swapaxes(cotangent, 1, 2)
    send, dispatch = pl.pallas_call(
        image_kernel,
        in_specs=[pl.BlockSpec(memory_space=pltpu.HBM)] * 3,
        scratch_shapes=[
            pltpu.VMEM(logits.shape, F32),
            pltpu.VMEM(patches.shape, BF16),
            pltpu.VMEM(cotangent.shape, BF16),
            pltpu.SemaphoreType.DMA((3,)),
        ],
        compiler_params=pltpu.CompilerParams(vmem_limit_bytes=24 * 1024 * 1024),
        out_shape=[
            shape((16, 8, 2 * width), BF16),
            shape((32, count), F32),
        ],
    )(*[pltpu.with_memory_space_constraint(a, pltpu.HBM) for a in (logits, patches, cotangent)])
    got = exchange(send, RING)
    send = call(
        regroup_kernel,
        shape((32, 8, deep), BF16),
        got,
        scratch=[pltpu.VMEM((64, deep), F32)],
    )
    rows = exchange(send, PLANE)
    send, grad_before, after, combine_term = call(
        expert_kernel,
        [
            shape((32, 8, deep // 2), BF16),
            shape((256, hidden), BF16),
            shape((256, hidden), BF16),
            shape((32, count), F32),
        ],
        rows,
        jnp.swapaxes(weight_in, 1, 2),
        weight_out,
        logits,
        cotangent,
        slot_outputs,
    )
    got = exchange(send, PLANE)
    grad_first, grad_second = call(
        weight_kernel,
        [shape((1, hidden, deep), BF16), shape((1, hidden, deep), BF16)],
        rows,
        grad_before,
        after,
    )
    send = call(partial_kernel, shape((16, 8, width), BF16), got)
    got = exchange(send, RING)
    send, slot_back = call(
        back_kernel,
        [shape((4, 32, count), BF16), shape((32, width), F32)],
        got,
        patches,
        dispatch,
        combine_term,
    )
    got = exchange(send, "tensor")
    grad_logits, send = call(
        logit_kernel,
        [shape((32, count), BF16), shape((32, 40, 128), BF16)],
        got,
        patches,
        scratch=[pltpu.VMEM((32, width), F32)],
    )
    got = exchange(send, PLANE)
    grad_patches = call(
        patch_kernel,
        shape((1, width, count), BF16),
        dispatch,
        slot_back,
        grad_logits,
        jnp.swapaxes(router, 0, 1),
    )
    got = exchange(call(add_kernel, shape((8, 40, 128), BF16), got), ("zh", "core"))
    grad_router = call(total_kernel, shape((32, width), F32), got)
    return (
        jnp.swapaxes(grad_patches, 1, 2),
        jnp.swapaxes(grad_router, 0, 1),
        jnp.swapaxes(grad_first, 1, 2),
        grad_second,
    )


def solution(mesh):
    split = Mesh(mesh.devices.reshape(4, 4, 4, 2, 4), ("dp", "y", "zh", "core", "tensor"))
    images = ("dp", "y", "zh", "core")
    experts = ("y", "zh", "core")
    return jax.shard_map(
        body,
        mesh=split,
        in_specs=(
            P(images, None, "tensor"),
            P("tensor", None),
            P(images, None, None),
            P(images, None, "tensor"),
            P(images, None, "tensor"),
            P(experts, None, ("dp", "tensor")),
            P(experts, ("dp", "tensor"), None),
        ),
        out_specs=(
            P(images, None, "tensor"),
            P("tensor", None),
            P(experts, None, ("dp", "tensor")),
            P(experts, ("dp", "tensor"), None),
        ),
        check_vma=False,
    )
```

```python
import jax
import jax.numpy as jnp
from jax import lax
from jax.experimental import pallas as pl
from jax.experimental.pallas import tpu as pltpu
from jax.sharding import Mesh
from jax.sharding import PartitionSpec as P

F32 = jnp.float32
BF16 = jnp.bfloat16
RING = ("tensor", "zh")
PLANE = ("dp", "y", "core")


def call(kernel, outs, *args, scratch=()):
    return pl.pallas_call(
        kernel,
        out_shape=outs,
        scratch_shapes=scratch,
        compiler_params=pltpu.CompilerParams(vmem_limit_bytes=24 * 1024 * 1024),
    )(*args)


def shape(dims, dtype):
    return jax.ShapeDtypeStruct(dims, dtype)


def pieces():
    return [(8 * zh + 2 * y, 8 * y + 2 * zh) for zh in range(4) for y in range(4)]


def rounded_dot(a, b, dims):
    return lax.dot_general(a, b, (dims, ((), ())), preferred_element_type=F32)


def soft(values, axis):
    top = jnp.exp(values - jnp.max(values, axis=axis, keepdims=True))
    return top / jnp.sum(top, axis=axis, keepdims=True)


def image_kernel(far_logits, far_patches, far_cotangent, send, dispatch, *scratch):
    logits, patches, cotangent, arrived = scratch
    copies = [
        pltpu.make_async_copy(source, target, arrived.at[i])
        for i, (source, target) in enumerate(
            [(far_logits, logits), (far_patches, patches), (far_cotangent, cotangent)]
        )
    ]
    for copy in copies:
        copy.start()
    copies[0].wait()
    for new, old in pieces():
        dispatch[new : new + 2, :] = logits[0, old : old + 2, :]
    values = dispatch[...]
    by_patch = soft(values, 1)
    by_slot = soft(values, 0)
    dispatch[...] = by_patch
    copies[1].wait()
    slot_in = rounded_dot(by_patch.astype(BF16), patches[0], ((1,), (1,)))
    copies[2].wait()
    slot_grad = rounded_dot(by_slot.astype(BF16), cotangent[0], ((1,), (1,)))
    width = slot_in.shape[1]
    for zh in range(4):
        ins = slot_in[8 * zh : 8 * zh + 8, :].astype(BF16)
        grads = slot_grad[8 * zh : 8 * zh + 8, :].astype(BF16)
        for zl in range(4):
            send[zh + 4 * zl, :, 0:width] = ins
            send[zh + 4 * zl, :, width : 2 * width] = grads


def regroup_kernel(got, send, stage):
    width = got.shape[2] // 2
    for zh in range(4):
        for zl in range(4):
            block = got[zh + 4 * zl].astype(F32)
            for kind in range(2):
                row = 32 * kind + 8 * zh
                stage[row : row + 8, width * zl : width * (zl + 1)] = block[
                    :, width * kind : width * (kind + 1)
                ]
    row = lax.broadcasted_iota(jnp.int32, (64, 64), 0)
    col = lax.broadcasted_iota(jnp.int32, (64, 64), 1)
    move = (row == (col % 8) * 8 + col // 8).astype(F32).astype(BF16)
    moved = jnp.dot(move, stage[...].astype(BF16), preferred_element_type=F32).astype(BF16)
    for x in range(4):
        send[8 * x : 8 * x + 8] = moved.reshape(8, 8, 4 * width)


GELU_SCALE = 0.7978845608028654
GELU_CUBE = 0.044715


def expert_kernel(
    rows, first, second, logits, cotangent, saved, send, grad_before, after, combine_term
):
    by_slot = soft(logits[0], 0)
    part = jnp.dot(saved[0], cotangent[0], preferred_element_type=F32)
    term = by_slot * (part - jnp.sum(by_slot * part, axis=0, keepdims=True))
    for new, old in pieces():
        combine_term[new : new + 2, :] = term[old : old + 2, :]
    both = rows[...].reshape(256, rows.shape[2])
    before = packed(rounded_dot(both, first[0], ((1,), (1,))), 0)
    grad_after = packed(rounded_dot(both, second[0], ((1,), (1,))), 1)
    square = before * before
    bent = jnp.tanh(GELU_SCALE * (before + GELU_CUBE * (before * square)))
    half = 0.5 * (1.0 + bent)
    slope = half + before * (
        (0.5 * GELU_SCALE) * ((1.0 - bent) * (1.0 + bent)) * (1.0 + (3.0 * GELU_CUBE) * square)
    )
    low = (grad_after * slope).astype(BF16)
    grad_before[...] = low
    after[...] = (before * half).astype(BF16)
    part = first.shape[2] // 2
    left = jnp.dot(low, first[0, :, :part], preferred_element_type=F32)
    right = jnp.dot(low, first[0, :, part:], preferred_element_type=F32)
    upper = is_upper(left.shape)
    send[0:16] = jnp.where(upper, left, pltpu.roll(right, 4, 0)).astype(BF16).reshape(16, 8, part)
    send[16:32] = jnp.where(upper, pltpu.roll(left, 124, 0), right).astype(BF16).reshape(16, 8, part)


def is_upper(dims):
    return lax.broadcasted_iota(jnp.int32, dims, 0) % 8 < 4


def packed(values, kind):
    head, tail = values[0:128, :], values[128:256, :]
    if kind == 0:
        return jnp.where(is_upper(head.shape), head, pltpu.roll(tail, 4, 0))
    return jnp.where(is_upper(head.shape), pltpu.roll(head, 124, 0), tail)


def spread(values, kind):
    values = values.astype(F32)
    upper = is_upper(values.shape)
    if kind == 0:
        head = jnp.where(upper, values, 0.0)
        tail = jnp.where(upper, pltpu.roll(values, 124, 0), 0.0)
    else:
        head = jnp.where(upper, 0.0, pltpu.roll(values, 4, 0))
        tail = jnp.where(upper, 0.0, values)
    return jnp.concatenate([head, tail], axis=0).astype(BF16)


def weight_kernel(rows, grad_before, after, grad_first, grad_second):
    both = rows[...].reshape(256, rows.shape[2])
    grad_first[0] = rounded_dot(spread(grad_before[...], 0), both, ((0,), (0,))).astype(BF16)
    grad_second[0] = rounded_dot(spread(after[...], 1), both, ((0,), (0,))).astype(BF16)


def partial_kernel(got, send):
    total = got[0:8].astype(F32)
    for x in range(1, 4):
        total = total + got[8 * x : 8 * x + 8].astype(F32)
    low = total.reshape(64, got.shape[2]).astype(BF16)
    row = lax.broadcasted_iota(jnp.int32, (64, 64), 0)
    col = lax.broadcasted_iota(jnp.int32, (64, 64), 1)
    move = (row == (col % 8) * 8 + col // 8).astype(F32).astype(BF16)
    moved = jnp.dot(move, low, preferred_element_type=F32).astype(BF16)
    width = send.shape[2]
    for zh in range(4):
        for zl in range(4):
            at = (zl // 2) * 32 + 8 * zh
            lane = (zl % 2) * width
            send[zh + 4 * zl] = moved[at : at + 8, lane : lane + width]


def back_kernel(got, patches, dispatch, combine_term, send, slot_back):
    for zh in range(4):
        total = got[zh].astype(F32)
        for zl in range(1, 4):
            total = total + got[zh + 4 * zl].astype(F32)
        slot_back[8 * zh : 8 * zh + 8, :] = total
    low = slot_back[...].astype(BF16)
    part = jnp.dot(low, patches[0], preferred_element_type=F32)
    by_patch = dispatch[...]
    grads = by_patch * (part - jnp.sum(by_patch * part, axis=1, keepdims=True))
    grads = (grads + combine_term[...]).astype(BF16)
    for zl in range(4):
        send[zl] = grads


def logit_kernel(got, patches, grad_logits, send, stage):
    total = got[0].astype(F32)
    for zl in range(1, 4):
        total = total + got[zl].astype(F32)
    low = total.astype(BF16)
    grad_logits[...] = low
    router = rounded_dot(low, patches[0], ((1,), (1,)))
    for new, old in pieces():
        stage[old : old + 2, :] = router[new : new + 2, :]
    for core in range(2):
        at = 16 * core
        rows = stage[at : at + 16, :].astype(BF16)
        rest = jnp.concatenate([stage[at : at + 8, 256:], stage[at + 8 : at + 16, 256:]], axis=1)
        rest = rest.astype(BF16)
        for j in range(16):
            send[2 * j + core, 0:16, :] = rows[:, 0:128]
            send[2 * j + core, 16:32, :] = rows[:, 128:256]
            send[2 * j + core, 32:40, :] = rest


def patch_kernel(dispatch, slot_back, grad_logits, router, grad_patches):
    new = lax.broadcasted_iota(jnp.int32, (32, 32), 0)
    old = lax.broadcasted_iota(jnp.int32, (32, 32), 1)
    move = (old == ((new // 2) % 4) * 8 + (new // 8) * 2 + new % 2).astype(F32).astype(BF16)
    columns = jnp.dot(move, router[...], preferred_element_type=F32)
    left = jnp.concatenate([dispatch[...], grad_logits[...].astype(F32)], axis=0).astype(BF16)
    right = jnp.concatenate([slot_back[...], columns], axis=0).astype(BF16)
    grad_patches[0] = rounded_dot(right, left, ((0,), (0,))).astype(BF16)


def add_kernel(got, send):
    total = got[0].astype(F32)
    for j in range(1, got.shape[0]):
        total = total + got[j].astype(F32)
    total = total.astype(send.dtype)
    for j in range(send.shape[0]):
        send[j] = total


def total_kernel(got, grad_router):
    for core in range(2):
        at = 16 * core
        total = got[core].astype(F32)
        for zh in range(1, 4):
            total = total + got[2 * zh + core].astype(F32)
        grad_router[at : at + 16, 0:128] = total[0:16, :]
        grad_router[at : at + 16, 128:256] = total[16:32, :]
        grad_router[at : at + 8, 256:320] = total[32:40, 0:64]
        grad_router[at + 8 : at + 16, 256:320] = total[32:40, 64:128]


def exchange(value, axes):
    return lax.all_to_all(value, axes, 0, 0, tiled=True)


def body(patches, router, logits, slot_outputs, cotangent, weight_in, weight_out):
    count, width = patches.shape[1:]
    deep = weight_in.shape[1]
    hidden = weight_in.shape[2]
    patches = jnp.swapaxes(patches, 1, 2)
    cotangent = jnp.swapaxes(cotangent, 1, 2)
    send, dispatch = pl.pallas_call(
        image_kernel,
        in_specs=[pl.BlockSpec(memory_space=pltpu.HBM)] * 3,
        scratch_shapes=[
            pltpu.VMEM(logits.shape, F32),
            pltpu.VMEM(patches.shape, BF16),
            pltpu.VMEM(cotangent.shape, BF16),
            pltpu.SemaphoreType.DMA((3,)),
        ],
        compiler_params=pltpu.CompilerParams(vmem_limit_bytes=24 * 1024 * 1024),
        out_shape=[
            shape((16, 8, 2 * width), BF16),
            shape((32, count), F32),
        ],
    )(*[pltpu.with_memory_space_constraint(a, pltpu.HBM) for a in (logits, patches, cotangent)])
    got = exchange(send, RING)
    send = call(
        regroup_kernel,
        shape((32, 8, deep), BF16),
        got,
        scratch=[pltpu.VMEM((64, deep), F32)],
    )
    rows = exchange(send, PLANE)
    send, grad_before, after, combine_term = call(
        expert_kernel,
        [
            shape((32, 8, deep // 2), BF16),
            shape((128, hidden), BF16),
            shape((128, hidden), BF16),
            shape((32, count), F32),
        ],
        rows,
        jnp.swapaxes(weight_in, 1, 2),
        weight_out,
        logits,
        cotangent,
        slot_outputs,
    )
    got = exchange(send, PLANE)
    grad_first, grad_second = call(
        weight_kernel,
        [shape((1, hidden, deep), BF16), shape((1, hidden, deep), BF16)],
        rows,
        grad_before,
        after,
    )
    send = call(partial_kernel, shape((16, 8, width), BF16), got)
    got = exchange(send, RING)
    send, slot_back = call(
        back_kernel,
        [shape((4, 32, count), BF16), shape((32, width), F32)],
        got,
        patches,
        dispatch,
        combine_term,
    )
    got = exchange(send, "tensor")
    grad_logits, send = call(
        logit_kernel,
        [shape((32, count), BF16), shape((32, 40, 128), BF16)],
        got,
        patches,
        scratch=[pltpu.VMEM((32, width), F32)],
    )
    got = exchange(send, PLANE)
    grad_patches = call(
        patch_kernel,
        shape((1, width, count), BF16),
        dispatch,
        slot_back,
        grad_logits,
        jnp.swapaxes(router, 0, 1),
    )
    got = exchange(call(add_kernel, shape((8, 40, 128), BF16), got), ("zh", "core"))
    grad_router = call(total_kernel, shape((32, width), F32), got)
    return (
        jnp.swapaxes(grad_patches, 1, 2),
        jnp.swapaxes(grad_router, 0, 1),
        jnp.swapaxes(grad_first, 1, 2),
        grad_second,
    )


def solution(mesh):
    split = Mesh(mesh.devices.reshape(4, 4, 4, 2, 4), ("dp", "y", "zh", "core", "tensor"))
    images = ("dp", "y", "zh", "core")
    experts = ("y", "zh", "core")
    return jax.shard_map(
        body,
        mesh=split,
        in_specs=(
            P(images, None, "tensor"),
            P("tensor", None),
            P(images, None, None),
            P(images, None, "tensor"),
            P(images, None, "tensor"),
            P(experts, None, ("dp", "tensor")),
            P(experts, ("dp", "tensor"), None),
        ),
        out_specs=(
            P(images, None, "tensor"),
            P("tensor", None),
            P(experts, None, ("dp", "tensor")),
            P(experts, ("dp", "tensor"), None),
        ),
        check_vma=False,
    )
```

```python
import jax
import jax.numpy as jnp
from jax import lax
from jax.experimental import pallas as pl
from jax.experimental.pallas import tpu as pltpu
from jax.sharding import Mesh
from jax.sharding import PartitionSpec as P

F32 = jnp.float32
BF16 = jnp.bfloat16
RING = ("zh", "tensor")
PLANE = ("dp", "y", "core")


def call(kernel, outs, *args, scratch=()):
    return pl.pallas_call(
        kernel,
        out_shape=outs,
        scratch_shapes=scratch,
        compiler_params=pltpu.CompilerParams(vmem_limit_bytes=24 * 1024 * 1024),
    )(*args)


def shape(dims, dtype):
    return jax.ShapeDtypeStruct(dims, dtype)


def pieces():
    return [(8 * zh + 2 * y, 8 * y + 2 * zh) for zh in range(4) for y in range(4)]


def rounded_dot(a, b, dims):
    return lax.dot_general(a, b, (dims, ((), ())), preferred_element_type=F32)


def soft(values, axis):
    top = jnp.exp(values - jnp.max(values, axis=axis, keepdims=True))
    return top / jnp.sum(top, axis=axis, keepdims=True)


def image_kernel(far_logits, far_patches, far_cotangent, send, dispatch, *scratch):
    logits, patches, cotangent, arrived = scratch
    copies = [
        pltpu.make_async_copy(source, target, arrived.at[i])
        for i, (source, target) in enumerate(
            [(far_logits, logits), (far_patches, patches), (far_cotangent, cotangent)]
        )
    ]
    for copy in copies:
        copy.start()
    copies[0].wait()
    for new, old in pieces():
        dispatch[new : new + 2, :] = logits[0, old : old + 2, :]
    values = dispatch[...]
    by_patch = soft(values, 1)
    by_slot = soft(values, 0)
    dispatch[...] = by_patch
    copies[1].wait()
    slot_in = rounded_dot(by_patch.astype(BF16), patches[0], ((1,), (1,)))
    copies[2].wait()
    slot_grad = rounded_dot(by_slot.astype(BF16), cotangent[0], ((1,), (1,)))
    width = slot_in.shape[1]
    for zh in range(4):
        ins = slot_in[8 * zh : 8 * zh + 8, :].astype(BF16)
        grads = slot_grad[8 * zh : 8 * zh + 8, :].astype(BF16)
        for zl in range(4):
            send[4 * zh + zl, :, 0:width] = ins
            send[4 * zh + zl, :, width : 2 * width] = grads


def regroup_kernel(got, send, stage):
    width = got.shape[2] // 2
    for zh in range(4):
        for zl in range(4):
            block = got[4 * zh + zl].astype(F32)
            for kind in range(2):
                row = 32 * kind + 8 * zh
                stage[row : row + 8, width * zl : width * (zl + 1)] = block[
                    :, width * kind : width * (kind + 1)
                ]
    row = lax.broadcasted_iota(jnp.int32, (64, 64), 0)
    col = lax.broadcasted_iota(jnp.int32, (64, 64), 1)
    move = (row == (col % 8) * 8 + col // 8).astype(F32).astype(BF16)
    moved = jnp.dot(move, stage[...].astype(BF16), preferred_element_type=F32).astype(BF16)
    for x in range(4):
        send[8 * x : 8 * x + 8] = moved.reshape(8, 8, 4 * width)


GELU_SCALE = 0.7978845608028654
GELU_CUBE = 0.044715


def expert_kernel(
    rows, first, second, logits, cotangent, saved, send, grad_before, after, combine_term
):
    by_slot = soft(logits[0], 0)
    part = jnp.dot(saved[0], cotangent[0], preferred_element_type=F32)
    term = by_slot * (part - jnp.sum(by_slot * part, axis=0, keepdims=True))
    for new, old in pieces():
        combine_term[new : new + 2, :] = term[old : old + 2, :]
    both = rows[...].reshape(256, rows.shape[2])
    before = packed(rounded_dot(both, first[0], ((1,), (1,))), 0)
    grad_after = packed(rounded_dot(both, second[0], ((1,), (1,))), 1)
    square = before * before
    bent = jnp.tanh(GELU_SCALE * (before + GELU_CUBE * (before * square)))
    half = 0.5 * (1.0 + bent)
    slope = half + before * (
        (0.5 * GELU_SCALE) * ((1.0 - bent) * (1.0 + bent)) * (1.0 + (3.0 * GELU_CUBE) * square)
    )
    low = (grad_after * slope).astype(BF16)
    grad_before[...] = low
    after[...] = (before * half).astype(BF16)
    part = first.shape[2] // 2
    left = jnp.dot(low, first[0, :, :part], preferred_element_type=F32)
    right = jnp.dot(low, first[0, :, part:], preferred_element_type=F32)
    upper = is_upper(left.shape)
    send[0:16] = jnp.where(upper, left, pltpu.roll(right, 4, 0)).astype(BF16).reshape(16, 8, part)
    send[16:32] = jnp.where(upper, pltpu.roll(left, 124, 0), right).astype(BF16).reshape(16, 8, part)


def is_upper(dims):
    return lax.broadcasted_iota(jnp.int32, dims, 0) % 8 < 4


def packed(values, kind):
    head, tail = values[0:128, :], values[128:256, :]
    if kind == 0:
        return jnp.where(is_upper(head.shape), head, pltpu.roll(tail, 4, 0))
    return jnp.where(is_upper(head.shape), pltpu.roll(head, 124, 0), tail)


def spread(values, kind):
    values = values.astype(F32)
    upper = is_upper(values.shape)
    if kind == 0:
        head = jnp.where(upper, values, 0.0)
        tail = jnp.where(upper, pltpu.roll(values, 124, 0), 0.0)
    else:
        head = jnp.where(upper, 0.0, pltpu.roll(values, 4, 0))
        tail = jnp.where(upper, 0.0, values)
    return jnp.concatenate([head, tail], axis=0).astype(BF16)


def weight_kernel(rows, grad_before, after, grad_first, grad_second):
    both = rows[...].reshape(256, rows.shape[2])
    grad_first[0] = rounded_dot(spread(grad_before[...], 0), both, ((0,), (0,))).astype(BF16)
    grad_second[0] = rounded_dot(spread(after[...], 1), both, ((0,), (0,))).astype(BF16)


def partial_kernel(got, send):
    total = got[0:8].astype(F32)
    for x in range(1, 4):
        total = total + got[8 * x : 8 * x + 8].astype(F32)
    low = total.reshape(64, got.shape[2]).astype(BF16)
    row = lax.broadcasted_iota(jnp.int32, (64, 64), 0)
    col = lax.broadcasted_iota(jnp.int32, (64, 64), 1)
    move = (row == (col % 8) * 8 + col // 8).astype(F32).astype(BF16)
    moved = jnp.dot(move, low, preferred_element_type=F32).astype(BF16)
    width = send.shape[2]
    for zh in range(4):
        for zl in range(4):
            at = (zl // 2) * 32 + 8 * zh
            lane = (zl % 2) * width
            send[4 * zh + zl] = moved[at : at + 8, lane : lane + width]


def back_kernel(got, patches, dispatch, combine_term, send, slot_back):
    for zh in range(4):
        total = got[4 * zh].astype(F32)
        for zl in range(1, 4):
            total = total + got[4 * zh + zl].astype(F32)
        slot_back[8 * zh : 8 * zh + 8, :] = total
    low = slot_back[...].astype(BF16)
    part = jnp.dot(low, patches[0], preferred_element_type=F32)
    by_patch = dispatch[...]
    grads = by_patch * (part - jnp.sum(by_patch * part, axis=1, keepdims=True))
    grads = (grads + combine_term[...]).astype(BF16)
    for zl in range(4):
        send[zl] = grads


def logit_kernel(got, patches, grad_logits, send, stage):
    total = got[0].astype(F32)
    for zl in range(1, 4):
        total = total + got[zl].astype(F32)
    low = total.astype(BF16)
    grad_logits[...] = low
    router = rounded_dot(low, patches[0], ((1,), (1,)))
    for new, old in pieces():
        stage[old : old + 2, :] = router[new : new + 2, :]
    for core in range(2):
        at = 16 * core
        rows = stage[at : at + 16, :].astype(BF16)
        rest = jnp.concatenate([stage[at : at + 8, 256:], stage[at + 8 : at + 16, 256:]], axis=1)
        rest = rest.astype(BF16)
        for j in range(16):
            send[2 * j + core, 0:16, :] = rows[:, 0:128]
            send[2 * j + core, 16:32, :] = rows[:, 128:256]
            send[2 * j + core, 32:40, :] = rest


def patch_kernel(dispatch, slot_back, grad_logits, router, grad_patches):
    new = lax.broadcasted_iota(jnp.int32, (32, 32), 0)
    old = lax.broadcasted_iota(jnp.int32, (32, 32), 1)
    move = (old == ((new // 2) % 4) * 8 + (new // 8) * 2 + new % 2).astype(F32).astype(BF16)
    columns = jnp.dot(move, router[...], preferred_element_type=F32)
    left = jnp.concatenate([dispatch[...], grad_logits[...].astype(F32)], axis=0).astype(BF16)
    right = jnp.concatenate([slot_back[...], columns], axis=0).astype(BF16)
    grad_patches[0] = rounded_dot(right, left, ((0,), (0,))).astype(BF16)


def add_kernel(got, send):
    total = got[0].astype(F32)
    for j in range(1, got.shape[0]):
        total = total + got[j].astype(F32)
    total = total.astype(send.dtype)
    for j in range(send.shape[0]):
        send[j] = total


def total_kernel(got, grad_router):
    for core in range(2):
        at = 16 * core
        total = got[core].astype(F32)
        for zh in range(1, 4):
            total = total + got[2 * zh + core].astype(F32)
        grad_router[at : at + 16, 0:128] = total[0:16, :]
        grad_router[at : at + 16, 128:256] = total[16:32, :]
        grad_router[at : at + 8, 256:320] = total[32:40, 0:64]
        grad_router[at + 8 : at + 16, 256:320] = total[32:40, 64:128]


def exchange(value, axes):
    return lax.all_to_all(value, axes, 0, 0, tiled=True)


def body(patches, router, logits, slot_outputs, cotangent, weight_in, weight_out):
    count, width = patches.shape[1:]
    deep = weight_in.shape[1]
    hidden = weight_in.shape[2]
    patches = jnp.swapaxes(patches, 1, 2)
    cotangent = jnp.swapaxes(cotangent, 1, 2)
    send, dispatch = pl.pallas_call(
        image_kernel,
        in_specs=[pl.BlockSpec(memory_space=pltpu.HBM)] * 3,
        scratch_shapes=[
            pltpu.VMEM(logits.shape, F32),
            pltpu.VMEM(patches.shape, BF16),
            pltpu.VMEM(cotangent.shape, BF16),
            pltpu.SemaphoreType.DMA((3,)),
        ],
        compiler_params=pltpu.CompilerParams(vmem_limit_bytes=24 * 1024 * 1024),
        out_shape=[
            shape((16, 8, 2 * width), BF16),
            shape((32, count), F32),
        ],
    )(*[pltpu.with_memory_space_constraint(a, pltpu.HBM) for a in (logits, patches, cotangent)])
    got = exchange(send, RING)
    send = call(
        regroup_kernel,
        shape((32, 8, deep), BF16),
        got,
        scratch=[pltpu.VMEM((64, deep), F32)],
    )
    rows = exchange(send, PLANE)
    send, grad_before, after, combine_term = call(
        expert_kernel,
        [
            shape((32, 8, deep // 2), BF16),
            shape((128, hidden), BF16),
            shape((128, hidden), BF16),
            shape((32, count), F32),
        ],
        rows,
        jnp.swapaxes(weight_in, 1, 2),
        weight_out,
        logits,
        cotangent,
        slot_outputs,
    )
    got = exchange(send, PLANE)
    grad_first, grad_second = call(
        weight_kernel,
        [shape((1, hidden, deep), BF16), shape((1, hidden, deep), BF16)],
        rows,
        grad_before,
        after,
    )
    send = call(partial_kernel, shape((16, 8, width), BF16), got)
    got = exchange(send, RING)
    send, slot_back = call(
        back_kernel,
        [shape((4, 32, count), BF16), shape((32, width), F32)],
        got,
        patches,
        dispatch,
        combine_term,
    )
    got = exchange(send, "tensor")
    grad_logits, send = call(
        logit_kernel,
        [shape((32, count), BF16), shape((32, 40, 128), BF16)],
        got,
        patches,
        scratch=[pltpu.VMEM((32, width), F32)],
    )
    got = exchange(send, PLANE)
    grad_patches = call(
        patch_kernel,
        shape((1, width, count), BF16),
        dispatch,
        slot_back,
        grad_logits,
        jnp.swapaxes(router, 0, 1),
    )
    got = exchange(call(add_kernel, shape((8, 40, 128), BF16), got), ("zh", "core"))
    grad_router = call(total_kernel, shape((32, width), F32), got)
    return (
        jnp.swapaxes(grad_patches, 1, 2),
        jnp.swapaxes(grad_router, 0, 1),
        jnp.swapaxes(grad_first, 1, 2),
        grad_second,
    )


def solution(mesh):
    split = Mesh(mesh.devices.reshape(4, 4, 4, 2, 4), ("dp", "y", "zh", "core", "tensor"))
    images = ("dp", "y", "zh", "core")
    experts = ("y", "zh", "core")
    return jax.shard_map(
        body,
        mesh=split,
        in_specs=(
            P(images, None, "tensor"),
            P("tensor", None),
            P(images, None, None),
            P(images, None, "tensor"),
            P(images, None, "tensor"),
            P(experts, None, ("dp", "tensor")),
            P(experts, ("dp", "tensor"), None),
        ),
        out_specs=(
            P(images, None, "tensor"),
            P("tensor", None),
            P(experts, None, ("dp", "tensor")),
            P(experts, ("dp", "tensor"), None),
        ),
        check_vma=False,
    )
```

```python
import jax
import jax.numpy as jnp
from jax import lax
from jax.experimental import pallas as pl
from jax.experimental.pallas import tpu as pltpu
from jax.sharding import Mesh
from jax.sharding import PartitionSpec as P

F32 = jnp.float32
BF16 = jnp.bfloat16
RING = ("zh", "tensor")
PLANE = ("dp", "y", "core")


def call(kernel, outs, *args, scratch=()):
    return pl.pallas_call(
        kernel,
        out_shape=outs,
        scratch_shapes=scratch,
        compiler_params=pltpu.CompilerParams(vmem_limit_bytes=24 * 1024 * 1024),
    )(*args)


def shape(dims, dtype):
    return jax.ShapeDtypeStruct(dims, dtype)


def pieces():
    return [(8 * zh + 2 * y, 8 * y + 2 * zh) for zh in range(4) for y in range(4)]


def rounded_dot(a, b, dims):
    return lax.dot_general(a, b, (dims, ((), ())), preferred_element_type=F32)


def soft(values, axis):
    top = jnp.exp(values - jnp.max(values, axis=axis, keepdims=True))
    return top / jnp.sum(top, axis=axis, keepdims=True)


def image_kernel(far_logits, far_patches, far_cotangent, send, dispatch, *scratch):
    logits, patches, cotangent, arrived = scratch
    copies = [
        pltpu.make_async_copy(source, target, arrived.at[i])
        for i, (source, target) in enumerate(
            [(far_logits, logits), (far_patches, patches), (far_cotangent, cotangent)]
        )
    ]
    for copy in copies:
        copy.start()
    copies[0].wait()
    for new, old in pieces():
        dispatch[new : new + 2, :] = logits[0, old : old + 2, :]
    values = dispatch[...]
    by_patch = soft(values, 1)
    by_slot = soft(values, 0)
    dispatch[...] = by_patch
    copies[1].wait()
    slot_in = rounded_dot(by_patch.astype(BF16), patches[0], ((1,), (1,)))
    copies[2].wait()
    slot_grad = rounded_dot(by_slot.astype(BF16), cotangent[0], ((1,), (1,)))
    width = slot_in.shape[1]
    for zh in range(4):
        ins = slot_in[8 * zh : 8 * zh + 8, :].astype(BF16)
        grads = slot_grad[8 * zh : 8 * zh + 8, :].astype(BF16)
        for zl in range(4):
            send[4 * zh + zl, :, 0:width] = ins
            send[4 * zh + zl, :, width : 2 * width] = grads


def regroup_kernel(got, send, stage):
    width = got.shape[2] // 2
    for zh in range(4):
        for zl in range(4):
            block = got[4 * zh + zl].astype(F32)
            for kind in range(2):
                row = 32 * kind + 8 * zh
                stage[row : row + 8, width * zl : width * (zl + 1)] = block[
                    :, width * kind : width * (kind + 1)
                ]
    row = lax.broadcasted_iota(jnp.int32, (64, 64), 0)
    col = lax.broadcasted_iota(jnp.int32, (64, 64), 1)
    move = (row == (col % 8) * 8 + col // 8).astype(F32).astype(BF16)
    moved = jnp.dot(move, stage[...].astype(BF16), preferred_element_type=F32).astype(BF16)
    for x in range(4):
        send[8 * x : 8 * x + 8] = moved.reshape(8, 8, 4 * width)


GELU_SCALE = 0.7978845608028654
GELU_CUBE = 0.044715


def expert_kernel(
    rows, first, second, logits, cotangent, saved, send, grad_before, after, combine_term
):
    by_slot = soft(logits[0], 0)
    part = jnp.dot(saved[0], cotangent[0], preferred_element_type=F32)
    term = by_slot * (part - jnp.sum(by_slot * part, axis=0, keepdims=True))
    for new, old in pieces():
        combine_term[new : new + 2, :] = term[old : old + 2, :]
    both = rows[...].reshape(256, rows.shape[2])
    before = packed(rounded_dot(both, first[0], ((1,), (1,))), 0)
    grad_after = packed(rounded_dot(both, second[0], ((1,), (1,))), 1)
    square = before * before
    bent = jnp.tanh(GELU_SCALE * (before + GELU_CUBE * (before * square)))
    half = 0.5 * (1.0 + bent)
    slope = half + before * (
        (0.5 * GELU_SCALE) * ((1.0 - bent) * (1.0 + bent)) * (1.0 + (3.0 * GELU_CUBE) * square)
    )
    low = (grad_after * slope).astype(BF16)
    grad_before[...] = low
    after[...] = (before * half).astype(BF16)
    part = first.shape[2] // 2
    left = jnp.dot(low, first[0, :, :part], preferred_element_type=F32)
    right = jnp.dot(low, first[0, :, part:], preferred_element_type=F32)
    upper = is_upper(left.shape)
    send[0:16] = jnp.where(upper, left, pltpu.roll(right, 4, 0)).astype(BF16).reshape(16, 8, part)
    send[16:32] = jnp.where(upper, pltpu.roll(left, 124, 0), right).astype(BF16).reshape(16, 8, part)


def is_upper(dims):
    return lax.broadcasted_iota(jnp.int32, dims, 0) % 8 < 4


def packed(values, kind):
    head, tail = values[0:128, :], values[128:256, :]
    if kind == 0:
        return jnp.where(is_upper(head.shape), head, pltpu.roll(tail, 4, 0))
    return jnp.where(is_upper(head.shape), pltpu.roll(head, 124, 0), tail)


def spread(values, kind):
    values = values.astype(F32)
    upper = is_upper(values.shape)
    if kind == 0:
        head = jnp.where(upper, values, 0.0)
        tail = jnp.where(upper, pltpu.roll(values, 124, 0), 0.0)
    else:
        head = jnp.where(upper, 0.0, pltpu.roll(values, 4, 0))
        tail = jnp.where(upper, 0.0, values)
    return jnp.concatenate([head, tail], axis=0).astype(BF16)


def weight_kernel(rows, grad_before, after, grad_first, grad_second):
    both = rows[...].reshape(256, rows.shape[2])
    grad_first[0] = rounded_dot(spread(grad_before[...], 0), both, ((0,), (0,))).astype(BF16)
    grad_second[0] = rounded_dot(spread(after[...], 1), both, ((0,), (0,))).astype(BF16)


def partial_kernel(got, send):
    total = got[0:8].astype(F32)
    for x in range(1, 4):
        total = total + got[8 * x : 8 * x + 8].astype(F32)
    low = total.reshape(64, got.shape[2]).astype(BF16)
    row = lax.broadcasted_iota(jnp.int32, (64, 64), 0)
    col = lax.broadcasted_iota(jnp.int32, (64, 64), 1)
    move = (row == (col % 8) * 8 + col // 8).astype(F32).astype(BF16)
    moved = jnp.dot(move, low, preferred_element_type=F32).astype(BF16)
    width = send.shape[2]
    for zh in range(4):
        for zl in range(4):
            at = (zl // 2) * 32 + 8 * zh
            lane = (zl % 2) * width
            send[4 * zh + zl] = moved[at : at + 8, lane : lane + width]


def back_kernel(got, patches, dispatch, combine_term, send, slot_back):
    for zh in range(4):
        total = got[4 * zh].astype(F32)
        for zl in range(1, 4):
            total = total + got[4 * zh + zl].astype(F32)
        slot_back[8 * zh : 8 * zh + 8, :] = total
    low = slot_back[...].astype(BF16)
    part = jnp.dot(low, patches[0], preferred_element_type=F32)
    by_patch = dispatch[...]
    grads = by_patch * (part - jnp.sum(by_patch * part, axis=1, keepdims=True))
    grads = grads + combine_term[...]
    rest = jnp.concatenate([grads[0:16, 512:], grads[16:32, 512:]], axis=1).astype(BF16)
    grads = grads.astype(BF16)
    for zl in range(4):
        for k in range(4):
            send[zl, 32 * k : 32 * k + 32, :] = grads[:, 128 * k : 128 * k + 128]
        send[zl, 128:144, :] = rest


def logit_kernel(got, patches, grad_logits, send, stage):
    total = got[0].astype(F32)
    for zl in range(1, 4):
        total = total + got[zl].astype(F32)
    rest = jnp.concatenate([total[128:144, 0:64], total[128:144, 64:128]], axis=0)
    blocks = [total[32 * k : 32 * k + 32, :] for k in range(4)]
    low = jnp.concatenate(blocks + [rest], axis=1).astype(BF16)
    grad_logits[...] = low
    router = rounded_dot(low, patches[0], ((1,), (1,)))
    for new, old in pieces():
        stage[old : old + 2, :] = router[new : new + 2, :]
    for core in range(2):
        at = 16 * core
        rows = stage[at : at + 16, :].astype(BF16)
        rest = jnp.concatenate([stage[at : at + 8, 256:], stage[at + 8 : at + 16, 256:]], axis=1)
        rest = rest.astype(BF16)
        for j in range(16):
            send[2 * j + core, 0:16, :] = rows[:, 0:128]
            send[2 * j + core, 16:32, :] = rows[:, 128:256]
            send[2 * j + core, 32:40, :] = rest


def patch_kernel(dispatch, slot_back, grad_logits, router, grad_patches):
    new = lax.broadcasted_iota(jnp.int32, (32, 32), 0)
    old = lax.broadcasted_iota(jnp.int32, (32, 32), 1)
    move = (old == ((new // 2) % 4) * 8 + (new // 8) * 2 + new % 2).astype(F32).astype(BF16)
    columns = jnp.dot(move, router[...], preferred_element_type=F32)
    left = jnp.concatenate([dispatch[...], grad_logits[...].astype(F32)], axis=0).astype(BF16)
    right = jnp.concatenate([slot_back[...], columns], axis=0).astype(BF16)
    grad_patches[0] = rounded_dot(right, left, ((0,), (0,))).astype(BF16)


def add_kernel(got, send):
    total = got[0].astype(F32)
    for j in range(1, got.shape[0]):
        total = total + got[j].astype(F32)
    total = total.astype(send.dtype)
    for j in range(send.shape[0]):
        send[j] = total


def total_kernel(got, grad_router):
    for core in range(2):
        at = 16 * core
        total = got[core].astype(F32)
        for zh in range(1, 4):
            total = total + got[2 * zh + core].astype(F32)
        grad_router[at : at + 16, 0:128] = total[0:16, :]
        grad_router[at : at + 16, 128:256] = total[16:32, :]
        grad_router[at : at + 8, 256:320] = total[32:40, 0:64]
        grad_router[at + 8 : at + 16, 256:320] = total[32:40, 64:128]


def exchange(value, axes):
    return lax.all_to_all(value, axes, 0, 0, tiled=True)


def body(patches, router, logits, slot_outputs, cotangent, weight_in, weight_out):
    count, width = patches.shape[1:]
    deep = weight_in.shape[1]
    hidden = weight_in.shape[2]
    patches = jnp.swapaxes(patches, 1, 2)
    cotangent = jnp.swapaxes(cotangent, 1, 2)
    send, dispatch = pl.pallas_call(
        image_kernel,
        in_specs=[pl.BlockSpec(memory_space=pltpu.HBM)] * 3,
        scratch_shapes=[
            pltpu.VMEM(logits.shape, F32),
            pltpu.VMEM(patches.shape, BF16),
            pltpu.VMEM(cotangent.shape, BF16),
            pltpu.SemaphoreType.DMA((3,)),
        ],
        compiler_params=pltpu.CompilerParams(vmem_limit_bytes=24 * 1024 * 1024),
        out_shape=[
            shape((16, 8, 2 * width), BF16),
            shape((32, count), F32),
        ],
    )(*[pltpu.with_memory_space_constraint(a, pltpu.HBM) for a in (logits, patches, cotangent)])
    got = exchange(send, RING)
    send = call(
        regroup_kernel,
        shape((32, 8, deep), BF16),
        got,
        scratch=[pltpu.VMEM((64, deep), F32)],
    )
    rows = exchange(send, PLANE)
    send, grad_before, after, combine_term = call(
        expert_kernel,
        [
            shape((32, 8, deep // 2), BF16),
            shape((128, hidden), BF16),
            shape((128, hidden), BF16),
            shape((32, count), F32),
        ],
        rows,
        jnp.swapaxes(weight_in, 1, 2),
        weight_out,
        logits,
        cotangent,
        slot_outputs,
    )
    got = exchange(send, PLANE)
    grad_first, grad_second = call(
        weight_kernel,
        [shape((1, hidden, deep), BF16), shape((1, hidden, deep), BF16)],
        rows,
        grad_before,
        after,
    )
    send = call(partial_kernel, shape((16, 8, width), BF16), got)
    got = exchange(send, RING)
    send, slot_back = call(
        back_kernel,
        [shape((4, 144, 128), BF16), shape((32, width), F32)],
        got,
        patches,
        dispatch,
        combine_term,
    )
    got = exchange(send, "tensor")
    grad_logits, send = call(
        logit_kernel,
        [shape((32, count), BF16), shape((32, 40, 128), BF16)],
        got,
        patches,
        scratch=[pltpu.VMEM((32, width), F32)],
    )
    got = exchange(send, PLANE)
    grad_patches = call(
        patch_kernel,
        shape((1, width, count), BF16),
        dispatch,
        slot_back,
        grad_logits,
        jnp.swapaxes(router, 0, 1),
    )
    got = exchange(call(add_kernel, shape((8, 40, 128), BF16), got), ("zh", "core"))
    grad_router = call(total_kernel, shape((32, width), F32), got)
    return (
        jnp.swapaxes(grad_patches, 1, 2),
        jnp.swapaxes(grad_router, 0, 1),
        jnp.swapaxes(grad_first, 1, 2),
        grad_second,
    )


def solution(mesh):
    split = Mesh(mesh.devices.reshape(4, 4, 4, 2, 4), ("dp", "y", "zh", "core", "tensor"))
    images = ("dp", "y", "zh", "core")
    experts = ("y", "zh", "core")
    return jax.shard_map(
        body,
        mesh=split,
        in_specs=(
            P(images, None, "tensor"),
            P("tensor", None),
            P(images, None, None),
            P(images, None, "tensor"),
            P(images, None, "tensor"),
            P(experts, None, ("dp", "tensor")),
            P(experts, ("dp", "tensor"), None),
        ),
        out_specs=(
            P(images, None, "tensor"),
            P("tensor", None),
            P(experts, None, ("dp", "tensor")),
            P(experts, ("dp", "tensor"), None),
        ),
        check_vma=False,
    )
```
